256 devices in a mesh: blk: 32 (over y, z), section: 4 (over x_hi, core), batch: 2 (over x_lo).
Axes of the slice: x: 4 (x_hi: 2, x_lo: 2; x = x_hi * 2 + x_lo), y: 4, z: 8, core: 2. Of those that a mesh axis runs over, the one named last changes fastest.
Arguments:
- latent: bfloat16 [16384, 3072], P(('batch', 'blk')), parts along dimension 0, may hold values from -48 to 48
- stale_kv: bfloat16 [2, 16384, 1536], P(None, ('batch', 'blk'), 'section'), parts along dimension 1, may hold values from -64 to 64
- text_kv: bfloat16 [2, 1024, 1536], P(None, 'batch', 'section'), parts along dimension 1, may hold values from -9 to 9
- text_count: int32 [2], P('batch'), parts along dimension 0, may hold values from 128 to 512
- timestep: int32 [2], P('batch'), parts along dimension 0, may hold values from 0 to 27
- modulation: bfloat16 [28, 9216], replicated, may hold values from -4 to 4
- w_qkv: bfloat16 [3072, 3, 1536], P(None, None, 'section'), may hold values from -0.109375 to 0.109375
- w_out: bfloat16 [1536, 3072], P('section'), may hold values from -0.15625 to 0.15625
- norm_gain: float32 [2, 128], replicated, may hold values from 1.2 to 2.6
Outputs:
- layer_out: bfloat16 [16384, 3072], P(('batch', 'blk'), 'section'), parts along dimension 0
- next_cache: bfloat16 [2, 16384, 1536], P(None, ('batch', 'blk'), 'section'), parts along dimension 1
The draws below stay inside these ranges and needn't reach their ends.
There are 2 independent parts, one for each index of `batch`. The reference program is written for one: setup_inputs(seed, part) draws one part's arguments, and reference() takes and returns one part's arrays. A program takes and returns all parts, laid end to end along the dimension named above; an argument that names none is the same for every part. Nothing has to cross between parts.
All inputs are finite; a program needn't handle non-finite values.
Results may differ from the reference program's by a relative error of at most 0.0075.
Values may be sent and summed in bfloat16 or wider, within the bound.
A program may use at most 128 MiB of HBM per device.

```python
import math
import jax
import jax.numpy as jnp
from jax import lax

D = 3072
HEADS = 12
HD = 128
TOK_DEV = 256
TXT = 512
STEPS = 28
INNER = 1536
IMG = 8192
N_BLK = 32


def draw_latent(key, part):
    key = jax.random.fold_in(key, 5)
    base_key, row_key, column_key = jax.random.split(key, 3)
    base_draw = jax.random.normal(base_key, (IMG, D), jnp.float32)
    row_scale = jnp.exp(jax.random.uniform(row_key, (IMG, 1), jnp.float32, math.log(0.3), math.log(3.0)))
    column_scale = jnp.exp(jax.random.uniform(column_key, (1, D), jnp.float32, math.log(0.5), math.log(2.0)))
    return jnp.clip(base_draw * row_scale * column_scale, -48.0, 48.0).astype(jnp.bfloat16)


def draw_stale_kv(key, part):
    key = jax.random.fold_in(key, 11)
    key_noise, value_noise = jax.random.split(key, 2)
    block_shape = (IMG, HEADS, HD)
    key_part = jnp.clip(1.6 * jax.random.normal(key_noise, block_shape, jnp.float32), -10.0, 10.0)
    value_part = jnp.clip(jax.random.normal(value_noise, block_shape, jnp.float32), -6.0, 6.0)
    return jnp.stack([key_part.reshape(IMG, HEADS * HD), value_part.reshape(IMG, HEADS * HD)]).astype(jnp.bfloat16)


def levels(own_key, extent, cuts, least, top_value):
    level, own = 1.0, jax.random.fold_in(own_key, 6)
    for position, parts in cuts:
        steps = jnp.exp(jax.random.uniform(jax.random.fold_in(own, position), (parts,), jnp.float32, least / len(cuts), top_value / len(cuts)))
        level = level * jnp.repeat(steps, extent[position] // parts).reshape([-1 if axis == position else 1 for axis in range(len(extent))])
    return level


def normal_values(rng, dims, scale, most, shards=(), kind=jnp.bfloat16):
    drawn = scale * jax.random.normal(rng, dims, jnp.float32)
    if shards:
        drawn = drawn * levels(rng, dims, shards, -0.22, 0.18)
    return jnp.clip(drawn, -most, most).astype(kind)


def setup_inputs(seed: int = 0, part: int = 0) -> dict:
    streams_of = jax.random.split(jax.random.key(seed), 10)
    part_splits = jax.random.split(jax.random.fold_in(streams_of[9], part), 10)
    return {
        "latent": draw_latent(jax.random.fold_in(jax.random.fold_in(streams_of[9], part), 71), part),
        "stale_kv": draw_stale_kv(jax.random.fold_in(jax.random.fold_in(streams_of[9], part), 71), part),
        "text_kv": normal_values(part_splits[2], (2, TXT, INNER), 1.5, 9.0, ((2, 4),)),
        "text_count": jax.random.randint(part_splits[3], (1,), TXT // 4, TXT + 1).astype(jnp.int32),
        "timestep": jax.random.randint(part_splits[4], (1,), 0, STEPS).astype(jnp.int32),
        "modulation": normal_values(streams_of[5], (STEPS, 3 * D), 0.7, 4.0),
        "w_qkv": normal_values(streams_of[6], (D, 3, INNER), D ** -0.5, 0.109375, ((2, 4),)),
        "w_out": normal_values(streams_of[7], (INNER, D), INNER ** -0.5, 0.15625, ((0, 4),)),
        "norm_gain": jnp.clip(jnp.exp(jax.random.uniform(streams_of[8], (2, HD), jnp.float32, math.log(1.2), math.log(2.6))), 1.2, 2.6),
    }


def head_norm(block, gain):
    square_mean = lax.optimization_barrier(jnp.mean(block * block, axis=-1, keepdims=True))
    return (block * lax.rsqrt(square_mean + 1e-06) * gain).astype(jnp.bfloat16)

def reference(latent, stale_kv, text_kv, text_count, timestep, modulation, w_qkv, w_out, norm_gain):
    inner = HEADS * HD
    mod_row = lax.dynamic_slice_in_dim(modulation, timestep[0], 1, 0)[0].astype(jnp.float32)
    shift_part = mod_row[:D]
    scale_part = mod_row[D:2 * D]
    gate_part = mod_row[2 * D:]
    hidden_float = latent.astype(jnp.float32)
    row_mean = lax.optimization_barrier(jnp.mean(hidden_float, axis=1, keepdims=True))
    centered = hidden_float - row_mean
    row_var = lax.optimization_barrier(jnp.mean(centered * centered, axis=1, keepdims=True))
    normed = (centered * lax.rsqrt(row_var + 1e-06) * (1.0 + scale_part) + shift_part).astype(jnp.bfloat16)
    projected = jnp.dot(normed, w_qkv.reshape(D, 3 * inner), preferred_element_type=jnp.float32)
    query_part = head_norm(projected[:, :inner].reshape(IMG, HEADS, HD), norm_gain[0])
    key_part = head_norm(projected[:, inner:2 * inner].reshape(IMG, HEADS, HD), norm_gain[1])
    value_part = projected[:, 2 * inner:].astype(jnp.bfloat16)
    fresh_pairs = jnp.stack([key_part.reshape(IMG, inner), value_part])
    text_valid = jnp.arange(TXT) < text_count[0]
    valid = jnp.concatenate([text_valid, jnp.ones((IMG,), bool)])

    def patch_attention(patch):
        start = (patch * TOK_DEV).astype(jnp.int32)
        own_rows = lax.dynamic_slice_in_dim(fresh_pairs, start, TOK_DEV, 1)
        image_pairs = lax.dynamic_update_slice_in_dim(stale_kv, own_rows, start, 1)
        all_pairs = jnp.concatenate([text_kv, image_pairs], axis=1).astype(jnp.float32)
        total_keys = all_pairs.shape[1]
        key_all = all_pairs[0].reshape(total_keys, HEADS, HD)
        value_all = all_pairs[1].reshape(total_keys, HEADS, HD)
        queries = lax.dynamic_slice_in_dim(query_part, start, TOK_DEV, 0).astype(jnp.float32)
        scores = jnp.einsum('qhd,khd->hqk', queries, key_all) * (1.0 / math.sqrt(HD))
        scores = jnp.where(valid[None, None, :], scores, -jnp.inf)
        top_score = lax.optimization_barrier(jnp.max(scores, axis=2, keepdims=True))
        expo = jnp.exp(scores - top_score)
        probs = (expo / lax.optimization_barrier(jnp.sum(expo, axis=2, keepdims=True))).astype(jnp.bfloat16)
        attended = jnp.einsum('hqk,khd->qhd', probs.astype(jnp.float32), value_all)
        return attended.astype(jnp.bfloat16).reshape(TOK_DEV, inner)
    attended_all = lax.map(patch_attention, jnp.arange(N_BLK, dtype=jnp.int32)).reshape(IMG, inner)
    branch = jnp.dot(attended_all, w_out, preferred_element_type=jnp.float32)
    layer_out = (hidden_float + gate_part * branch).astype(jnp.bfloat16)
    return (layer_out, fresh_pairs)
```

```python
import functools
import math

import jax
import jax.numpy as jnp
from jax import lax
from jax.experimental import pallas as pl
from jax.experimental.pallas import tpu as pltpu
from jax.sharding import PartitionSpec as P

MESH = pl.DeviceIdType.MESH
HD = 128
NY, NZ = 4, 8
HALF = NZ // 2
HEADS = 3
SECTIONS = 4
TOK = 256
TXT = 512
WIDTH = 3072
COLS = WIDTH // SECTIONS
PIECES = 2
ROWS = TOK // PIECES
SCORE_SCALE = math.log2(math.e) / math.sqrt(HD)


def kernel(
    text_count, timestep, modulation, gain, latent, stale, text, w_qkv, w_out,
    layer_out, next_cache,
    lat_v, normed, w_v, text_v, kv, fresh, q_all, acc, top, den,
    o_send, o_recv, s_send, s_recv, att, w_all, branch,
    kv_ss, kv_rs, q_ss, q_rs, w_ss, w_rs, o_ss, o_rs, s_ss, s_rs, a_ss, a_rs,
    lat_sem, wq_sem, text_sem, own_sem, cache_sem, wo_sem,
):
    blk = lax.axis_index("blk")
    sec = lax.axis_index("section")
    y, z = blk // NZ, blk % NZ

    def at_y(k):
        return {"blk": ((y + k + NY) % NY) * NZ + z}

    def at_sec(j):
        return {"section": (sec + j) % SECTIONS}

    right = {"blk": y * NZ + (z + 1) % NZ}
    left = {"blk": y * NZ + (z + NZ - 1) % NZ}
    friends = [right, left] + [at_y(k) for k in range(1, NY)] + [at_sec(j) for j in range(1, SECTIONS)]
    barrier = pltpu.get_barrier_semaphore()
    for friend in friends:
        pl.semaphore_signal(barrier, inc=1, device_id=friend, device_id_type=MESH)

    def head_cols(h):
        return pl.ds(h * HD, HD)

    lat_copy = pltpu.make_async_copy(latent, lat_v, lat_sem)
    lat_copy.start()
    wq_copies = [pltpu.make_async_copy(w_qkv.at[c], w_v.at[c], wq_sem.at[c]) for c in range(3)]
    for copy in wq_copies:
        copy.start()
    text_copies = [
        pltpu.make_async_copy(text.at[:, :, head_cols(h)], text_v.at[h], text_sem.at[h]) for h in range(HEADS)
    ]
    own_copies = [
        pltpu.make_async_copy(stale.at[:, :, head_cols(h)], kv.at[0, h], own_sem.at[h]) for h in range(HEADS)
    ]
    wo_copy = pltpu.make_async_copy(
        w_out.at[:, :, pl.ds(pl.multiple_of(sec * COLS, COLS), COLS)], w_all.at[:, sec], wo_sem
    )
    for copy in text_copies + own_copies + [wo_copy]:
        copy.start()

    pl.semaphore_wait(barrier, len(friends))

    def ring(h, d, side, piece):
        rows = pl.ds(piece * ROWS, ROWS)
        into = d if side == 0 else NZ - d
        source = stale.at[:, rows, head_cols(h)] if d == 1 else kv.at[d - 1 if side == 0 else NZ - d + 1, h, :, rows, :]
        return pltpu.make_async_remote_copy(
            src_ref=source,
            dst_ref=kv.at[into, h, :, rows, :],
            send_sem=kv_ss.at[side, d, h, piece],
            recv_sem=kv_rs.at[side, d, h, piece],
            device_id=right if side == 0 else left,
            device_id_type=MESH,
        )

    def parts(d):
        return [
            (side, piece) for piece in range(PIECES) for side in range(2)
            if d < HALF or (piece < PIECES // 2) == (side == 0)
        ]

    def arrive(h, d):
        onward = parts(d + 1) if d < HALF else []
        for side, piece in parts(d):
            ring(h, d, side, piece).wait_recv()
            if (side, piece) in onward:
                ring(h, d + 1, side, piece).start()

    for h in range(HEADS):
        for side, piece in parts(1):
            ring(h, 1, side, piece).start()

    def w_send(j):
        to = lax.rem(sec + j, SECTIONS)
        return pltpu.make_async_remote_copy(
            src_ref=w_out.at[:, :, pl.ds(pl.multiple_of(to * COLS, COLS), COLS)],
            dst_ref=w_all.at[:, sec],
            send_sem=w_ss.at[j],
            recv_sem=w_rs.at[j],
            device_id=at_sec(j),
            device_id_type=MESH,
        )

    for j in range(1, SECTIONS):
        w_send(j).start()

    steps = lax.broadcasted_iota(jnp.int32, modulation.shape, 0)
    mod_row = jnp.sum(
        jnp.where(steps == timestep[0], modulation[...].astype(jnp.float32), 0.0), axis=0, keepdims=True
    )
    shift, scale, gate = (mod_row[:, i * WIDTH : (i + 1) * WIDTH] for i in range(3))
    scale = 1.0 + scale
    lat_copy.wait()

    chunk = 16

    def norm_rows(i, _):
        rows = pl.ds(pl.multiple_of(i * chunk, chunk), chunk)
        x = lat_v[rows, :].astype(jnp.float32)
        centered = x - jnp.mean(x, axis=1, keepdims=True)
        var = jnp.mean(centered * centered, axis=1, keepdims=True)
        normed[rows, :] = (centered * lax.rsqrt(var + 1e-06) * scale + shift).astype(jnp.bfloat16)
        return 0

    lax.fori_loop(0, TOK // chunk, norm_rows, 0)

    def project(c):
        wq_copies[c].wait()
        return jnp.dot(normed[...], w_v[c], preferred_element_type=jnp.float32)

    def head_norm(block, g):
        square = jnp.mean(block * block, axis=-1, keepdims=True)
        return (block * lax.rsqrt(square + 1e-06) * g).astype(jnp.bfloat16)

    def q_send(h, k):
        return pltpu.make_async_remote_copy(
            src_ref=q_all.at[h, 0],
            dst_ref=q_all.at[h, k],
            send_sem=q_ss.at[h, k],
            recv_sem=q_rs.at[h, k],
            device_id=at_y(k),
            device_id_type=MESH,
        )

    projected = project(0)
    for h in range(HEADS):
        q_all[h, 0] = head_norm(projected[:, h * HD : (h + 1) * HD], gain[0:1, :])
        for k in range(1, NY):
            q_send(h, k).start()
    arrive(0, 1)
    projected = project(1)
    for h in range(HEADS):
        fresh[h, 0] = head_norm(projected[:, h * HD : (h + 1) * HD], gain[1:2, :])
    arrive(1, 1)
    projected = project(2)
    for h in range(HEADS):
        fresh[h, 1] = projected[:, h * HD : (h + 1) * HD].astype(jnp.bfloat16)
    arrive(2, 1)
    cache_copies = [
        pltpu.make_async_copy(fresh.at[h], next_cache.at[:, :, head_cols(h)], cache_sem.at[h]) for h in range(HEADS)
    ]
    for copy in cache_copies:
        copy.start()

    def scores(q, keys):
        s = lax.dot_general(q, keys, (((1,), (1,)), ((), ())), preferred_element_type=jnp.float32)
        return s * SCORE_SCALE

    def attend(h, k, blocks, first):
        q = q_all[h, k]
        logits = []
        for keys, _, live in blocks:
            s = scores(q, keys)
            if live is not None:
                s = jnp.where(live, s, -jnp.inf)
            logits.append(s)
        best = functools.reduce(jnp.maximum, [jnp.max(s, axis=1, keepdims=True) for s in logits])
        if not first:
            before = top[h, k][:, 0:1]
            best = jnp.maximum(before, best)
        total = None
        for s, (_, values, _) in zip(logits, blocks):
            p = jnp.exp2(s - best).astype(jnp.bfloat16)
            ones = jnp.ones(values.shape, jnp.bfloat16)
            part = jnp.dot(p, jnp.concatenate([values, ones], axis=1), preferred_element_type=jnp.float32)
            total = part if total is None else total + part
        new_acc, new_den = total[:, :HD], total[:, HD:]
        if not first:
            fade = jnp.exp2(before - best)
            new_acc = new_acc + acc[h, k] * fade
            new_den = new_den + den[h, k] * fade
        acc[h, k] = new_acc
        den[h, k] = new_den
        top[h, k] = jnp.broadcast_to(best, (TOK, HD))

    def own_step(h):
        live = lax.broadcasted_iota(jnp.int32, (TOK, TXT), 1) < text_count[0]
        attend(h, 0, [(fresh[h, 0], fresh[h, 1], None), (text_v[h, 0], text_v[h, 1], live)], True)

        def one(k, _):
            attend(h, k, [(kv[0, h, 0], kv[0, h, 1], None)], True)
            return 0

        lax.fori_loop(1, NY, one, 0)

    def pair_step(h, d):
        def one(k, _):
            attend(h, k, [(kv[i, h, 0], kv[i, h, 1], None) for i in (d, NZ - d)], False)
            return 0

        lax.fori_loop(0, NY, one, 0)

    for copy in text_copies + own_copies:
        copy.wait()
    for h in range(HEADS):
        for k in range(1, NY):
            q_send(h, k).wait_recv()

    for d in range(2, HALF):
        def ring_step(h, _, d=d):
            arrive(h, d)
            if d == 2:
                own_step(h)
            pair_step(h, d - 1)
            return 0

        lax.fori_loop(0, HEADS, ring_step, 0)

    def last_pairs(h, _):
        pair_step(h, HALF - 1)
        return 0

    lax.fori_loop(0, HEADS, last_pairs, 0)

    def o_copies(h, k):
        return [
            pltpu.make_async_remote_copy(
                src_ref=a.at[h, k],
                dst_ref=b.at[h, k],
                send_sem=ss.at[h, k],
                recv_sem=rs.at[h, k],
                device_id=at_y(-k),
                device_id_type=MESH,
            )
            for a, b, ss, rs in ((o_send, o_recv, o_ss, o_rs), (s_send, s_recv, s_ss, s_rs))
        ]

    def opposite(h, k):
        attend(h, k, [(kv[HALF, h, 0], kv[HALF, h, 1], None)], False)

    def finish(h):
        arrive(h, HALF)

        def one(k, _):
            opposite(h, k)
            total = den[h, k]
            o_send[h, k] = (acc[h, k] / total).astype(jnp.bfloat16)
            lse = top[h, k] + jnp.log2(total)
            for i in range(TOK // HD):
                s_send[h, k, :, i * HD : (i + 1) * HD] = lse[i * HD : (i + 1) * HD, :].T[0:8, :]
            for copy in o_copies(h, k):
                copy.start()
            return 0

        lax.fori_loop(1, NY, one, 0)
        opposite(h, 0)

    def a_send(h, j):
        return pltpu.make_async_remote_copy(
            src_ref=att.at[h, sec],
            dst_ref=att.at[h, sec],
            send_sem=a_ss.at[h, j],
            recv_sem=a_rs.at[h, j],
            device_id=at_sec(j),
            device_id_type=MESH,
        )

    def merge(h):
        total = den[h, 0]
        outs = [acc[h, 0] / total]
        lses = [top[h, 0] + jnp.log2(total)]
        for k in range(1, NY):
            for copy in o_copies(h, k):
                copy.wait_recv()
            outs.append(o_recv[h, k].astype(jnp.float32))
            stat = s_recv[h, k]
            lses.append(
                jnp.concatenate(
                    [
                        jnp.broadcast_to(stat[0:1, i * HD : (i + 1) * HD], (HD, HD)).T
                        for i in range(TOK // HD)
                    ],
                    axis=0,
                )
            )
        best = functools.reduce(jnp.maximum, lses)
        weights = [jnp.exp2(lse - best) for lse in lses]
        blend = functools.reduce(jnp.add, [o * w for o, w in zip(outs, weights)])
        att[h, sec] = (blend / functools.reduce(jnp.add, weights)).astype(jnp.bfloat16)
        for j in range(1, SECTIONS):
            a_send(h, j).start()

    def out_project(h):
        for j in range(1, SECTIONS):
            a_send(h, j).wait_recv()
        heads = jnp.concatenate([att[h, s] for s in range(SECTIONS)], axis=1)
        return jnp.dot(heads, w_all[h].reshape(SECTIONS * HD, COLS), preferred_element_type=jnp.float32)

    finish(0)
    finish(1)
    merge(0)
    finish(2)
    merge(1)
    wo_copy.wait()
    for j in range(1, SECTIONS):
        w_send(j).wait_recv()
    branch[...] = out_project(0)
    merge(2)
    branch[...] += out_project(1)
    columns = pl.ds(pl.multiple_of(sec * COLS, COLS), COLS)
    steps = lax.broadcasted_iota(jnp.int32, (modulation.shape[0], COLS), 0)
    gate_cols = modulation[:, pl.ds(pl.multiple_of(2 * WIDTH + sec * COLS, COLS), COLS)].astype(jnp.float32)
    gate_row = jnp.sum(jnp.where(steps == timestep[0], gate_cols, 0.0), axis=0, keepdims=True)
    summed = branch[...] + out_project(2)
    layer_out[...] = (lat_v[:, columns].astype(jnp.float32) + gate_row * summed).astype(jnp.bfloat16)

    for h in range(HEADS):
        for d in range(1, HALF + 1):
            for side, piece in parts(d):
                ring(h, d, side, piece).wait_send()
        for k in range(1, NY):
            q_send(h, k).wait_send()
            for copy in o_copies(h, k):
                copy.wait_send()
        for j in range(1, SECTIONS):
            a_send(h, j).wait_send()
    for j in range(1, SECTIONS):
        w_send(j).wait_send()
    for copy in cache_copies:
        copy.wait()


def local(latent, stale_kv, text_kv, text_count, timestep, modulation, w_qkv, w_out, norm_gain):
    vmem = pl.BlockSpec(memory_space=pltpu.VMEM)
    smem = pl.BlockSpec(memory_space=pltpu.SMEM)
    hbm = pl.BlockSpec(memory_space=pl.ANY)
    bf16, f32 = jnp.bfloat16, jnp.float32
    dma = pltpu.SemaphoreType.DMA
    return pl.pallas_call(
        kernel,
        out_shape=(
            jax.ShapeDtypeStruct((TOK, COLS), bf16),
            jax.ShapeDtypeStruct((2, TOK, HEADS * HD), bf16),
        ),
        in_specs=[smem, smem, vmem, vmem, hbm, hbm, hbm, hbm, hbm],
        out_specs=(vmem, hbm),
        scratch_shapes=[
            pltpu.VMEM((TOK, WIDTH), bf16),
            pltpu.VMEM((TOK, WIDTH), bf16),
            pltpu.VMEM((3, WIDTH, HEADS * HD), bf16),
            pltpu.VMEM((HEADS, 2, TXT, HD), bf16),
            pltpu.VMEM((NZ, HEADS, 2, TOK, HD), bf16),
            pltpu.VMEM((HEADS, 2, TOK, HD), bf16),
            pltpu.VMEM((HEADS, NY, TOK, HD), bf16),
            pltpu.VMEM((HEADS, NY, TOK, HD), f32),
            pltpu.VMEM((HEADS, NY, TOK, HD), f32),
            pltpu.VMEM((HEADS, NY, TOK, HD), f32),
            pltpu.VMEM((HEADS, NY, TOK, HD), bf16),
            pltpu.VMEM((HEADS, NY, TOK, HD), bf16),
            pltpu.VMEM((HEADS, NY, 8, TOK), f32),
            pltpu.VMEM((HEADS, NY, 8, TOK), f32),
            pltpu.VMEM((HEADS, SECTIONS, TOK, HD), bf16),
            pltpu.VMEM((HEADS, SECTIONS, HD, COLS), bf16),
            pltpu.VMEM((TOK, COLS), f32),
            dma((2, HALF + 1, HEADS, PIECES)), dma((2, HALF + 1, HEADS, PIECES)),
            dma((HEADS, NY)), dma((HEADS, NY)),
            dma((SECTIONS,)), dma((SECTIONS,)),
            dma((HEADS, NY)), dma((HEADS, NY)),
            dma((HEADS, NY)), dma((HEADS, NY)),
            dma((HEADS, SECTIONS)), dma((HEADS, SECTIONS)),
            dma, dma((3,)), dma((HEADS,)), dma((HEADS,)), dma((HEADS,)), dma,
        ],
        compiler_params=pltpu.CompilerParams(
            collective_id=1, has_side_effects=True, vmem_limit_bytes=52 << 20
        ),
    )(
        text_count, timestep, modulation, norm_gain, latent, stale_kv, text_kv,
        w_qkv.transpose(1, 0, 2), w_out.reshape(HEADS, HD, WIDTH),
    )


def solution(mesh):
    in_specs = (
        P(("batch", "blk"), None),
        P(None, ("batch", "blk"), "section"),
        P(None, "batch", "section"),
        P("batch"),
        P("batch"),
        P(),
        P(None, None, "section"),
        P("section", None),
        P(),
    )
    out_specs = (P(("batch", "blk"), "section"), P(None, ("batch", "blk"), "section"))
    return jax.shard_map(local, mesh=mesh, in_specs=in_specs, out_specs=out_specs, check_vma=False)
```

```python
import functools
import math

import jax
import jax.numpy as jnp
from jax import lax
from jax.experimental import pallas as pl
from jax.experimental.pallas import tpu as pltpu
from jax.sharding import PartitionSpec as P

MESH = pl.DeviceIdType.MESH
HD = 128
NY, NZ = 4, 8
HALF = NZ // 2
HEADS = 3
SECTIONS = 4
TOK = 256
TXT = 512
STEPS = 28
WIDTH = 3072
COLS = WIDTH // SECTIONS
PIECES = 2
ROWS = TOK // PIECES
PARTS = 2
PART = TOK // PARTS
EXTRA = 16
SCORE_SCALE = math.log2(math.e) / math.sqrt(HD)


def kernel(
    text_count, timestep, mod_in, gain_in, latent, stale, text, w_qkv, w_out,
    layer_out, next_cache,
    modulation, gain, lat_v, normed, w_v, text_v, kv, fresh, q_all, acc, top, den,
    o_send, o_recv, att, w_all, branch,
    kv_ss, kv_rs, q_ss, q_rs, w_ss, w_rs, o_ss, o_rs, a_ss, a_rs,
    mod_sem, gain_sem, lat_sem, wq_sem, text_sem, own_sem, cache_sem, wo_sem,
):
    blk = lax.axis_index("blk")
    sec = lax.axis_index("section")
    y, z = blk // NZ, blk % NZ

    def at_y(k):
        return {"blk": ((y + k + NY) % NY) * NZ + z}

    def at_sec(j):
        return {"section": (sec + j) % SECTIONS}

    right = {"blk": y * NZ + (z + 1) % NZ}
    left = {"blk": y * NZ + (z + NZ - 1) % NZ}
    friends = [right, left] + [at_y(k) for k in range(1, NY)] + [at_sec(j) for j in range(1, SECTIONS)]
    barrier = pltpu.get_barrier_semaphore()
    for friend in friends:
        pl.semaphore_signal(barrier, inc=1, device_id=friend, device_id_type=MESH)

    def head_cols(h):
        return pl.ds(h * HD, HD)

    own_copies = [
        pltpu.make_async_copy(stale.at[:, :, head_cols(h)], kv.at[0, h], own_sem.at[h]) for h in range(HEADS)
    ]
    for copy in own_copies:
        copy.start()
    pl.semaphore_wait(barrier, len(friends))
    for copy in own_copies:
        copy.wait()

    def ring(h, d, side, piece):
        rows = pl.ds(piece * ROWS, ROWS)
        into = d if side == 0 else NZ - d
        source = kv.at[0 if d == 1 else d - 1 if side == 0 else NZ - d + 1, h, :, rows, :]
        return pltpu.make_async_remote_copy(
            src_ref=source,
            dst_ref=kv.at[into, h, :, rows, :],
            send_sem=kv_ss.at[side, d, h, piece],
            recv_sem=kv_rs.at[side, d, h, piece],
            device_id=right if side == 0 else left,
            device_id_type=MESH,
        )

    def parts(d):
        return [
            (side, piece) for piece in range(PIECES) for side in range(2)
            if d < HALF or (piece < PIECES // 2) == (side == 0)
        ]

    def arrive(h, d):
        onward = parts(d + 1) if d < HALF else []
        for side, piece in parts(d):
            ring(h, d, side, piece).wait_recv()
            if (side, piece) in onward:
                ring(h, d + 1, side, piece).start()

    for h in range(HEADS):
        for side, piece in parts(1):
            ring(h, 1, side, piece).start()

    def w_send(j):
        to = lax.rem(sec + j, SECTIONS)
        return pltpu.make_async_remote_copy(
            src_ref=w_out.at[:, :, pl.ds(pl.multiple_of(to * COLS, COLS), COLS)],
            dst_ref=w_all.at[:, sec],
            send_sem=w_ss.at[j],
            recv_sem=w_rs.at[j],
            device_id=at_sec(j),
            device_id_type=MESH,
        )

    mod_copy = pltpu.make_async_copy(mod_in, modulation, mod_sem)
    gain_copy = pltpu.make_async_copy(gain_in, gain, gain_sem)
    lat_copy = pltpu.make_async_copy(latent, lat_v, lat_sem)
    for copy in (lat_copy, mod_copy, gain_copy):
        copy.start()
    wq_copies = [pltpu.make_async_copy(w_qkv.at[c], w_v.at[c], wq_sem.at[c]) for c in range(3)]
    for copy in wq_copies:
        copy.start()
    text_copies = [
        pltpu.make_async_copy(text.at[:, :, head_cols(h)], text_v.at[h], text_sem.at[h]) for h in range(HEADS)
    ]
    wo_copy = pltpu.make_async_copy(
        w_out.at[:, :, pl.ds(pl.multiple_of(sec * COLS, COLS), COLS)], w_all.at[:, sec], wo_sem
    )
    for copy in text_copies + [wo_copy]:
        copy.start()

    for j in range(1, SECTIONS):
        w_send(j).start()

    mod_copy.wait()
    def pick_row(rows):
        steps = lax.broadcasted_iota(jnp.int32, rows.shape, 0)
        return jnp.sum(jnp.where(steps == timestep[0], rows.astype(jnp.float32), 0.0), axis=0, keepdims=True)

    shift = pick_row(modulation[:, :WIDTH])
    scale = 1.0 + pick_row(modulation[:, WIDTH : 2 * WIDTH])
    lat_copy.wait()
    gain_copy.wait()

    chunk = 16

    def norm_rows(i, _):
        rows = pl.ds(pl.multiple_of(i * chunk, chunk), chunk)
        x = lat_v[rows, :].astype(jnp.float32)
        centered = x - jnp.mean(x, axis=1, keepdims=True)
        var = jnp.mean(centered * centered, axis=1, keepdims=True)
        normed[rows, :] = (centered * lax.rsqrt(var + 1e-06) * scale + shift).astype(jnp.bfloat16)
        return 0

    lax.fori_loop(0, TOK // chunk, norm_rows, 0)

    def project(c):
        wq_copies[c].wait()
        return jnp.dot(normed[...], w_v[c], preferred_element_type=jnp.float32)

    def head_norm(block, g):
        square = jnp.mean(block * block, axis=-1, keepdims=True)
        return (block * lax.rsqrt(square + 1e-06) * g).astype(jnp.bfloat16)

    def q_send(h, k):
        return pltpu.make_async_remote_copy(
            src_ref=q_all.at[h, 0:TOK, :],
            dst_ref=q_all.at[h, k * TOK : (k + 1) * TOK, :],
            send_sem=q_ss.at[h, k],
            recv_sem=q_rs.at[h, k],
            device_id=at_y(k),
            device_id_type=MESH,
        )

    projected = project(0)
    for h in range(HEADS):
        q_all[h, 0:TOK, :] = head_norm(projected[:, h * HD : (h + 1) * HD], gain[0:1, :])
        for k in range(1, NY):
            q_send(h, k).start()
    arrive(0, 1)
    projected = project(1)
    for h in range(HEADS):
        fresh[h, 0] = head_norm(projected[:, h * HD : (h + 1) * HD], gain[1:2, :])
    arrive(1, 1)
    projected = project(2)
    for h in range(HEADS):
        fresh[h, 1] = projected[:, h * HD : (h + 1) * HD].astype(jnp.bfloat16)
    arrive(2, 1)
    cache_copies = [
        pltpu.make_async_copy(fresh.at[h], next_cache.at[:, :, head_cols(h)], cache_sem.at[h]) for h in range(HEADS)
    ]
    for copy in cache_copies:
        copy.start()

    def attend(h, low, high, blocks, first):
        q = q_all[h, low:high, :]
        logits = []
        for keys, _, live in blocks:
            s = lax.dot_general(keys, q, (((1,), (1,)), ((), ())), preferred_element_type=jnp.float32)
            logits.append(s if live is None else jnp.where(live, s, -jnp.inf))
        best = functools.reduce(jnp.maximum, [jnp.max(s, axis=0, keepdims=True) for s in logits])
        if not first:
            before = top[h, 0:1, low:high]
            best = jnp.maximum(before, best)
        new_acc = new_den = None
        for s, (_, values, _) in zip(logits, blocks):
            p = jnp.exp2((s - best) * SCORE_SCALE)
            part_den = jnp.sum(p, axis=0, keepdims=True)
            part = lax.dot_general(
                values, p.astype(jnp.bfloat16), (((0,), (0,)), ((), ())), preferred_element_type=jnp.float32
            )
            new_acc = part if new_acc is None else new_acc + part
            new_den = part_den if new_den is None else new_den + part_den
        if not first:
            fade = jnp.exp2((before - best) * SCORE_SCALE)
            new_acc = new_acc + acc[h, :, low:high] * fade
            new_den = new_den + den[h, 0:1, low:high] * fade
        acc[h, :, low:high] = new_acc
        den[h, 0:1, low:high] = new_den
        top[h, 0:1, low:high] = best

    def own_step(h):
        for k in range(1, NY):
            q_send(h, k).wait_recv()
        live = lax.broadcasted_iota(jnp.int32, (TXT, TOK), 0) < text_count[0]
        attend(h, 0, TOK, [(fresh[h, 0], fresh[h, 1], None), (text_v[h, 0], text_v[h, 1], live)], True)
        attend(h, TOK, NY * TOK, [(kv[0, h, 0], kv[0, h, 1], None)], True)

    def pair_step(h, d):
        slots = (d, NZ - d) if d < HALF else (d,)
        attend(h, 0, NY * TOK, [(kv[i, h, 0], kv[i, h, 1], None) for i in slots], False)

    def o_copy(h, k, part):
        return pltpu.make_async_remote_copy(
            src_ref=o_send.at[h, k, part],
            dst_ref=o_recv.at[h, k, part],
            send_sem=o_ss.at[h, k, part],
            recv_sem=o_rs.at[h, k, part],
            device_id=at_y(-k),
            device_id_type=MESH,
        )

    def slot_result(h, k, part):
        start = k * TOK + part * PART
        cols = slice(start, start + PART)
        total = den[h, 0:1, cols]
        return acc[h, :, cols] * (1.0 / total), top[h, 0:1, cols] * SCORE_SCALE + jnp.log2(total)

    def rounded(v):
        return v.astype(jnp.bfloat16).astype(jnp.float32)

    def finish(h):
        for part in range(PARTS):
            for k in (2, 1, 3):
                out, lse = slot_result(h, k, part)
                rest = lse - rounded(lse)
                row = lax.broadcasted_iota(jnp.int32, (EXTRA, PART), 0)
                terms = jnp.where(row == 0, lse, jnp.where(row == 1, rest, rest - rounded(rest)))
                o_send[h, k, part, 0:HD, :] = out.astype(jnp.bfloat16)
                o_send[h, k, part, HD:, :] = terms.astype(jnp.bfloat16)
                o_copy(h, k, part).start()

    def a_send(h, j, part):
        return pltpu.make_async_remote_copy(
            src_ref=att.at[h, part, sec],
            dst_ref=att.at[h, part, sec],
            send_sem=a_ss.at[h, j, part],
            recv_sem=a_rs.at[h, j, part],
            device_id=at_sec(j),
            device_id_type=MESH,
        )

    def merge(h, part):
        results = [slot_result(h, 0, part)]
        for k in (1, 3, 2):
            o_copy(h, k, part).wait_recv()
            terms = o_recv[h, k, part, HD:, :].astype(jnp.float32)
            lse = terms[0:1, :] + terms[1:2, :] + terms[2:3, :]
            results.append((o_recv[h, k, part, 0:HD, :].astype(jnp.float32), lse))
        best = functools.reduce(jnp.maximum, [lse for _, lse in results])
        weights = [jnp.exp2(lse - best) for _, lse in results]
        inverse = 1.0 / functools.reduce(jnp.add, weights)
        blend = functools.reduce(jnp.add, [o * (w * inverse) for (o, _), w in zip(results, weights)])
        att[h, part, sec] = blend.astype(jnp.bfloat16)
        for j in (2, 1, 3):
            a_send(h, j, part).start()

    def out_project(h, part):
        for j in (1, 3, 2):
            a_send(h, j, part).wait_recv()
        return lax.dot_general(
            att[h, part].reshape(SECTIONS * HD, PART),
            w_all[h].reshape(SECTIONS * HD, COLS),
            (((0,), (0,)), ((), ())),
            preferred_element_type=jnp.float32,
        )

    for copy in text_copies:
        copy.wait()
    own_step(0)
    own_step(1)
    own_step(2)
    arrive(0, 2)
    pair_step(0, 1)
    arrive(1, 2)
    pair_step(1, 1)
    pair_step(2, 1)
    arrive(0, 3)
    pair_step(0, 2)
    pair_step(0, 3)
    arrive(2, 2)
    pair_step(1, 2)
    arrive(0, 4)
    pair_step(0, 4)
    finish(0)
    arrive(1, 3)
    pair_step(2, 2)
    pair_step(1, 3)
    arrive(2, 3)
    merge(0, 0)
    merge(0, 1)
    pair_step(2, 3)
    arrive(1, 4)
    pair_step(1, 4)
    finish(1)
    arrive(2, 4)
    pair_step(2, 4)
    finish(2)
    merge(1, 0)
    merge(1, 1)
    wo_copy.wait()
    for j in range(1, SECTIONS):
        w_send(j).wait_recv()
    columns = pl.ds(pl.multiple_of(sec * COLS, COLS), COLS)
    gate_row = pick_row(modulation[:, pl.ds(pl.multiple_of(2 * WIDTH + sec * COLS, COLS), COLS)])
    for part in range(PARTS):
        branch[part] = out_project(0, part)
    for part in range(PARTS):
        merge(2, part)
    for part in range(PARTS):
        branch[part] += out_project(1, part)
    for part in range(PARTS):
        rows = slice(part * PART, (part + 1) * PART)
        summed = branch[part] + out_project(2, part)
        layer_out[rows, :] = (lat_v[rows, columns].astype(jnp.float32) + gate_row * summed).astype(jnp.bfloat16)

    for h in range(HEADS):
        for d in range(1, HALF + 1):
            for side, piece in parts(d):
                ring(h, d, side, piece).wait_send()
        for k in range(1, NY):
            q_send(h, k).wait_send()
            for part in range(PARTS):
                o_copy(h, k, part).wait_send()
        for j in range(1, SECTIONS):
            for part in range(PARTS):
                a_send(h, j, part).wait_send()
    for j in range(1, SECTIONS):
        w_send(j).wait_send()
    for copy in cache_copies:
        copy.wait()


def local(latent, stale_kv, text_kv, text_count, timestep, modulation, w_qkv, w_out, norm_gain):
    vmem = pl.BlockSpec(memory_space=pltpu.VMEM)
    smem = pl.BlockSpec(memory_space=pltpu.SMEM)
    hbm = pl.BlockSpec(memory_space=pltpu.HBM)
    bf16, f32 = jnp.bfloat16, jnp.float32
    dma = pltpu.SemaphoreType.DMA
    return pl.pallas_call(
        kernel,
        out_shape=(
            jax.ShapeDtypeStruct((TOK, COLS), bf16),
            jax.ShapeDtypeStruct((2, TOK, HEADS * HD), bf16),
        ),
        in_specs=[smem, smem, hbm, hbm, hbm, hbm, hbm, hbm, hbm],
        out_specs=(vmem, hbm),
        scratch_shapes=[
            pltpu.VMEM((STEPS, 3 * WIDTH), bf16),
            pltpu.VMEM((2, HD), f32),
            pltpu.VMEM((TOK, WIDTH), bf16),
            pltpu.VMEM((TOK, WIDTH), bf16),
            pltpu.VMEM((3, WIDTH, HEADS * HD), bf16),
            pltpu.VMEM((HEADS, 2, TXT, HD), bf16),
            pltpu.VMEM((NZ, HEADS, 2, TOK, HD), bf16),
            pltpu.VMEM((HEADS, 2, TOK, HD), bf16),
            pltpu.VMEM((HEADS, NY * TOK, HD), bf16),
            pltpu.VMEM((HEADS, HD, NY * TOK), f32),
            pltpu.VMEM((HEADS, 8, NY * TOK), f32),
            pltpu.VMEM((HEADS, 8, NY * TOK), f32),
            pltpu.VMEM((HEADS, NY, PARTS, HD + EXTRA, PART), bf16),
            pltpu.VMEM((HEADS, NY, PARTS, HD + EXTRA, PART), bf16),
            pltpu.VMEM((HEADS, PARTS, SECTIONS, HD, PART), bf16),
            pltpu.VMEM((HEADS, SECTIONS, HD, COLS), bf16),
            pltpu.VMEM((PARTS, PART, COLS), f32),
            dma((2, HALF + 1, HEADS, PIECES)), dma((2, HALF + 1, HEADS, PIECES)),
            dma((HEADS, NY)), dma((HEADS, NY)),
            dma((SECTIONS,)), dma((SECTIONS,)),
            dma((HEADS, NY, PARTS)), dma((HEADS, NY, PARTS)),
            dma((HEADS, SECTIONS, PARTS)), dma((HEADS, SECTIONS, PARTS)),
            dma, dma, dma, dma((3,)), dma((HEADS,)), dma((HEADS,)), dma((HEADS,)), dma,
        ],
        compiler_params=pltpu.CompilerParams(
            collective_id=1, has_side_effects=True, vmem_limit_bytes=52 << 20
        ),
    )(
        text_count, timestep, modulation, norm_gain, latent, stale_kv, text_kv,
        w_qkv.transpose(1, 0, 2), w_out.reshape(HEADS, HD, WIDTH),
    )


def solution(mesh):
    in_specs = (
        P(("batch", "blk"), None),
        P(None, ("batch", "blk"), "section"),
        P(None, "batch", "section"),
        P("batch"),
        P("batch"),
        P(),
        P(None, None, "section"),
        P("section", None),
        P(),
    )
    out_specs = (P(("batch", "blk"), "section"), P(None, ("batch", "blk"), "section"))
    return jax.shard_map(local, mesh=mesh, in_specs=in_specs, out_specs=out_specs, check_vma=False)
```

```python
import functools
import math

import jax
import jax.numpy as jnp
from jax import lax
from jax.experimental import pallas as pl
from jax.experimental.pallas import tpu as pltpu
from jax.sharding import PartitionSpec as P

MESH = pl.DeviceIdType.MESH
HD = 128
NY, NZ = 4, 8
HALF = NZ // 2
HEADS = 3
SECTIONS = 4
TOK = 256
TXT = 512
STEPS = 28
WIDTH = 3072
COLS = WIDTH // SECTIONS
PIECES = 2
ROWS = TOK // PIECES
PARTS = 2
PART = TOK // PARTS
EXTRA = 16
SCORE_SCALE = math.log2(math.e) / math.sqrt(HD)


def kernel(
    text_count, timestep, mod_in, gain_in, latent, stale, text, w_qkv, w_out,
    layer_out, next_cache,
    modulation, gain, lat_v, normed, w_v, text_v, kv, fresh, q_all, acc, top, den,
    o_send, o_recv, att, w_all, branch,
    kv_ss, kv_rs, q_ss, q_rs, w_ss, w_rs, o_ss, o_rs, a_ss, a_rs,
    mod_sem, gain_sem, lat_sem, wq_sem, text_sem, own_sem, cache_sem, wo_sem,
):
    blk = lax.axis_index("blk")
    sec = lax.axis_index("section")
    y, z = blk // NZ, blk % NZ

    def at_y(k):
        return {"blk": ((y + k + NY) % NY) * NZ + z}

    def at_sec(j):
        return {"section": (sec + j) % SECTIONS}

    right = {"blk": y * NZ + (z + 1) % NZ}
    left = {"blk": y * NZ + (z + NZ - 1) % NZ}
    friends = [right, left] + [at_y(k) for k in range(1, NY)] + [at_sec(j) for j in range(1, SECTIONS)]
    barrier = pltpu.get_barrier_semaphore()
    for friend in friends:
        pl.semaphore_signal(barrier, inc=1, device_id=friend, device_id_type=MESH)

    def head_cols(h):
        return pl.ds(h * HD, HD)

    own_copies = [
        pltpu.make_async_copy(stale.at[:, :, head_cols(h)], kv.at[0, h], own_sem.at[h]) for h in range(HEADS)
    ]
    for copy in own_copies:
        copy.start()
    pl.semaphore_wait(barrier, len(friends))
    for copy in own_copies:
        copy.wait()

    def ring(h, d, side, piece):
        rows = pl.ds(piece * ROWS, ROWS)
        into = d if side == 0 else NZ - d
        source = kv.at[0 if d == 1 else d - 1 if side == 0 else NZ - d + 1, h, :, rows, :]
        return pltpu.make_async_remote_copy(
            src_ref=source,
            dst_ref=kv.at[into, h, :, rows, :],
            send_sem=kv_ss.at[side, d, h, piece],
            recv_sem=kv_rs.at[side, d, h, piece],
            device_id=right if side == 0 else left,
            device_id_type=MESH,
        )

    def parts(d):
        return [(side, side if first else 1 - side) for first in (True, False)[: 2 if d < HALF else 1] for side in range(2)]

    def arrive(h, d):
        onward = parts(d + 1) if d < HALF else []
        for side, piece in parts(d):
            ring(h, d, side, piece).wait_recv()
            if (side, piece) in onward:
                ring(h, d + 1, side, piece).start()

    for h in range(HEADS):
        for side, piece in parts(1):
            ring(h, 1, side, piece).start()

    def w_send(j):
        to = lax.rem(sec + j, SECTIONS)
        return pltpu.make_async_remote_copy(
            src_ref=w_out.at[:, :, pl.ds(pl.multiple_of(to * COLS, COLS), COLS)],
            dst_ref=w_all.at[:, sec],
            send_sem=w_ss.at[j],
            recv_sem=w_rs.at[j],
            device_id=at_sec(j),
            device_id_type=MESH,
        )

    mod_copy = pltpu.make_async_copy(mod_in, modulation, mod_sem)
    gain_copy = pltpu.make_async_copy(gain_in, gain, gain_sem)
    lat_copy = pltpu.make_async_copy(latent, lat_v, lat_sem)
    for copy in (lat_copy, mod_copy, gain_copy):
        copy.start()
    wq_copies = [pltpu.make_async_copy(w_qkv.at[c], w_v.at[c], wq_sem.at[c]) for c in range(3)]
    for copy in wq_copies:
        copy.start()
    text_copies = [
        pltpu.make_async_copy(text.at[:, :, head_cols(h)], text_v.at[h], text_sem.at[h]) for h in range(HEADS)
    ]
    wo_copy = pltpu.make_async_copy(
        w_out.at[:, :, pl.ds(pl.multiple_of(sec * COLS, COLS), COLS)], w_all.at[:, sec], wo_sem
    )
    for copy in text_copies + [wo_copy]:
        copy.start()

    for j in range(1, SECTIONS):
        w_send(j).start()

    mod_copy.wait()
    def pick_row(rows):
        steps = lax.broadcasted_iota(jnp.int32, rows.shape, 0)
        return jnp.sum(jnp.where(steps == timestep[0], rows.astype(jnp.float32), 0.0), axis=0, keepdims=True)

    shift = pick_row(modulation[:, :WIDTH])
    scale = 1.0 + pick_row(modulation[:, WIDTH : 2 * WIDTH])
    lat_copy.wait()
    gain_copy.wait()

    chunk = 16

    def norm_rows(i, _):
        rows = pl.ds(pl.multiple_of(i * chunk, chunk), chunk)
        x = lat_v[rows, :].astype(jnp.float32)
        centered = x - jnp.mean(x, axis=1, keepdims=True)
        var = jnp.mean(centered * centered, axis=1, keepdims=True)
        normed[rows, :] = (centered * lax.rsqrt(var + 1e-06) * scale + shift).astype(jnp.bfloat16)
        return 0

    lax.fori_loop(0, TOK // chunk, norm_rows, 0)

    def project(c):
        wq_copies[c].wait()
        return jnp.dot(normed[...], w_v[c], preferred_element_type=jnp.float32)

    def head_norm(block, g):
        square = jnp.mean(block * block, axis=-1, keepdims=True)
        return (block * lax.rsqrt(square + 1e-06) * g).astype(jnp.bfloat16)

    def q_send(h, k):
        return pltpu.make_async_remote_copy(
            src_ref=q_all.at[h, 0:TOK, :],
            dst_ref=q_all.at[h, k * TOK : (k + 1) * TOK, :],
            send_sem=q_ss.at[h, k],
            recv_sem=q_rs.at[h, k],
            device_id=at_y(k),
            device_id_type=MESH,
        )

    projected = project(0)
    for h in range(HEADS):
        q_all[h, 0:TOK, :] = head_norm(projected[:, h * HD : (h + 1) * HD], gain[0:1, :])
        for k in range(1, NY):
            q_send(h, k).start()
    arrive(0, 1)
    projected = project(1)
    for h in range(HEADS):
        fresh[h, 0] = head_norm(projected[:, h * HD : (h + 1) * HD], gain[1:2, :])
    arrive(1, 1)
    projected = project(2)
    for h in range(HEADS):
        fresh[h, 1] = projected[:, h * HD : (h + 1) * HD].astype(jnp.bfloat16)
    arrive(2, 1)
    cache_copies = [
        pltpu.make_async_copy(fresh.at[h], next_cache.at[:, :, head_cols(h)], cache_sem.at[h]) for h in range(HEADS)
    ]
    for copy in cache_copies:
        copy.start()

    def attend(h, low, high, blocks, first):
        q = q_all[h, low:high, :]
        logits = []
        for keys, _, live in blocks:
            s = lax.dot_general(keys, q, (((1,), (1,)), ((), ())), preferred_element_type=jnp.float32)
            logits.append(s if live is None else jnp.where(live, s, -jnp.inf))
        best = functools.reduce(jnp.maximum, [jnp.max(s, axis=0, keepdims=True) for s in logits])
        if not first:
            before = top[h, 0:1, low:high]
            best = jnp.maximum(before, best)
        new_acc = new_den = None
        for s, (_, values, _) in zip(logits, blocks):
            p = jnp.exp2((s - best) * SCORE_SCALE)
            part_den = jnp.sum(p, axis=0, keepdims=True)
            part = lax.dot_general(
                values, p.astype(jnp.bfloat16), (((0,), (0,)), ((), ())), preferred_element_type=jnp.float32
            )
            new_acc = part if new_acc is None else new_acc + part
            new_den = part_den if new_den is None else new_den + part_den
        if not first:
            fade = jnp.exp2((before - best) * SCORE_SCALE)
            new_acc = new_acc + acc[h, :, low:high] * fade
            new_den = new_den + den[h, 0:1, low:high] * fade
        acc[h, :, low:high] = new_acc
        den[h, 0:1, low:high] = new_den
        top[h, 0:1, low:high] = best

    def own_step(h):
        for k in range(1, NY):
            q_send(h, k).wait_recv()
        live = lax.broadcasted_iota(jnp.int32, (TXT, TOK), 0) < text_count[0]
        attend(h, 0, TOK, [(fresh[h, 0], fresh[h, 1], None), (text_v[h, 0], text_v[h, 1], live)], True)
        attend(h, TOK, NY * TOK, [(kv[0, h, 0], kv[0, h, 1], None)], True)

    def pair_step(h, d):
        attend(h, 0, NY * TOK, [(kv[i, h, 0], kv[i, h, 1], None) for i in (d, NZ - d)], False)

    def o_copy(h, k, part):
        return pltpu.make_async_remote_copy(
            src_ref=o_send.at[h, k, part],
            dst_ref=o_recv.at[h, k, part],
            send_sem=o_ss.at[h, k, part],
            recv_sem=o_rs.at[h, k, part],
            device_id=at_y(-k),
            device_id_type=MESH,
        )

    def slot_result(h, k, part):
        start = k * TOK + part * PART
        cols = slice(start, start + PART)
        total = den[h, 0:1, cols]
        return acc[h, :, cols] * (1.0 / total), top[h, 0:1, cols] * SCORE_SCALE + jnp.log2(total)

    def rounded(v):
        return v.astype(jnp.bfloat16).astype(jnp.float32)

    def finish(h):
        for part in range(PARTS):
            for k in (2, 1, 3):
                out, lse = slot_result(h, k, part)
                rest = lse - rounded(lse)
                row = lax.broadcasted_iota(jnp.int32, (EXTRA, PART), 0)
                terms = jnp.where(row == 0, lse, jnp.where(row == 1, rest, rest - rounded(rest)))
                o_send[h, k, part, 0:HD, :] = out.astype(jnp.bfloat16)
                o_send[h, k, part, HD:, :] = terms.astype(jnp.bfloat16)
                o_copy(h, k, part).start()

    def last_step(h):
        block = [(kv[HALF, h, 0], kv[HALF, h, 1], None)]
        attend(h, TOK, NY * TOK, block, False)
        finish(h)
        attend(h, 0, TOK, block, False)

    def a_send(h, j, part):
        return pltpu.make_async_remote_copy(
            src_ref=att.at[h, part, sec],
            dst_ref=att.at[h, part, sec],
            send_sem=a_ss.at[h, j, part],
            recv_sem=a_rs.at[h, j, part],
            device_id=at_sec(j),
            device_id_type=MESH,
        )

    def merge(h, part):
        results = [slot_result(h, 0, part)]
        for k in (1, 3, 2):
            o_copy(h, k, part).wait_recv()
            terms = o_recv[h, k, part, HD:, :].astype(jnp.float32)
            lse = terms[0:1, :] + terms[1:2, :] + terms[2:3, :]
            results.append((o_recv[h, k, part, 0:HD, :].astype(jnp.float32), lse))
        best = functools.reduce(jnp.maximum, [lse for _, lse in results])
        weights = [jnp.exp2(lse - best) for _, lse in results]
        inverse = 1.0 / functools.reduce(jnp.add, weights)
        blend = functools.reduce(jnp.add, [o * (w * inverse) for (o, _), w in zip(results, weights)])
        att[h, part, sec] = blend.astype(jnp.bfloat16)
        for j in (2, 1, 3):
            a_send(h, j, part).start()

    def out_project(h, part):
        for j in (1, 3, 2):
            a_send(h, j, part).wait_recv()
        return lax.dot_general(
            att[h, part].reshape(SECTIONS * HD, PART),
            w_all[h].reshape(SECTIONS * HD, COLS),
            (((0,), (0,)), ((), ())),
            preferred_element_type=jnp.float32,
        )

    for copy in text_copies:
        copy.wait()
    own_step(0)
    own_step(1)
    own_step(2)
    arrive(0, 2)
    pair_step(0, 1)
    arrive(1, 2)
    pair_step(1, 1)
    pair_step(2, 1)
    arrive(0, 3)
    pair_step(0, 2)
    pair_step(0, 3)
    arrive(2, 2)
    pair_step(1, 2)
    arrive(0, 4)
    last_step(0)
    arrive(1, 3)
    pair_step(2, 2)
    pair_step(1, 3)
    arrive(2, 3)
    merge(0, 0)
    merge(0, 1)
    pair_step(2, 3)
    arrive(1, 4)
    last_step(1)
    arrive(2, 4)
    last_step(2)
    merge(1, 0)
    merge(1, 1)
    wo_copy.wait()
    for j in range(1, SECTIONS):
        w_send(j).wait_recv()
    columns = pl.ds(pl.multiple_of(sec * COLS, COLS), COLS)
    gate_row = pick_row(modulation[:, pl.ds(pl.multiple_of(2 * WIDTH + sec * COLS, COLS), COLS)])
    for part in range(PARTS):
        branch[part] = out_project(0, part)
    for part in range(PARTS):
        merge(2, part)
    for part in range(PARTS):
        branch[part] += out_project(1, part)
    for part in range(PARTS):
        rows = slice(part * PART, (part + 1) * PART)
        summed = branch[part] + out_project(2, part)
        layer_out[rows, :] = (lat_v[rows, columns].astype(jnp.float32) + gate_row * summed).astype(jnp.bfloat16)

    for h in range(HEADS):
        for d in range(1, HALF + 1):
            for side, piece in parts(d):
                ring(h, d, side, piece).wait_send()
        for k in range(1, NY):
            q_send(h, k).wait_send()
            for part in range(PARTS):
                o_copy(h, k, part).wait_send()
        for j in range(1, SECTIONS):
            for part in range(PARTS):
                a_send(h, j, part).wait_send()
    for j in range(1, SECTIONS):
        w_send(j).wait_send()
    for copy in cache_copies:
        copy.wait()


def local(latent, stale_kv, text_kv, text_count, timestep, modulation, w_qkv, w_out, norm_gain):
    vmem = pl.BlockSpec(memory_space=pltpu.VMEM)
    smem = pl.BlockSpec(memory_space=pltpu.SMEM)
    hbm = pl.BlockSpec(memory_space=pltpu.HBM)
    bf16, f32 = jnp.bfloat16, jnp.float32
    dma = pltpu.SemaphoreType.DMA
    return pl.pallas_call(
        kernel,
        out_shape=(
            jax.ShapeDtypeStruct((TOK, COLS), bf16),
            jax.ShapeDtypeStruct((2, TOK, HEADS * HD), bf16),
        ),
        in_specs=[smem, smem, hbm, hbm, hbm, hbm, hbm, hbm, hbm],
        out_specs=(vmem, hbm),
        scratch_shapes=[
            pltpu.VMEM((STEPS, 3 * WIDTH), bf16),
            pltpu.VMEM((2, HD), f32),
            pltpu.VMEM((TOK, WIDTH), bf16),
            pltpu.VMEM((TOK, WIDTH), bf16),
            pltpu.VMEM((3, WIDTH, HEADS * HD), bf16),
            pltpu.VMEM((HEADS, 2, TXT, HD), bf16),
            pltpu.VMEM((NZ, HEADS, 2, TOK, HD), bf16),
            pltpu.VMEM((HEADS, 2, TOK, HD), bf16),
            pltpu.VMEM((HEADS, NY * TOK, HD), bf16),
            pltpu.VMEM((HEADS, HD, NY * TOK), f32),
            pltpu.VMEM((HEADS, 8, NY * TOK), f32),
            pltpu.VMEM((HEADS, 8, NY * TOK), f32),
            pltpu.VMEM((HEADS, NY, PARTS, HD + EXTRA, PART), bf16),
            pltpu.VMEM((HEADS, NY, PARTS, HD + EXTRA, PART), bf16),
            pltpu.VMEM((HEADS, PARTS, SECTIONS, HD, PART), bf16),
            pltpu.VMEM((HEADS, SECTIONS, HD, COLS), bf16),
            pltpu.VMEM((PARTS, PART, COLS), f32),
            dma((2, HALF + 1, HEADS, PIECES)), dma((2, HALF + 1, HEADS, PIECES)),
            dma((HEADS, NY)), dma((HEADS, NY)),
            dma((SECTIONS,)), dma((SECTIONS,)),
            dma((HEADS, NY, PARTS)), dma((HEADS, NY, PARTS)),
            dma((HEADS, SECTIONS, PARTS)), dma((HEADS, SECTIONS, PARTS)),
            dma, dma, dma, dma((3,)), dma((HEADS,)), dma((HEADS,)), dma((HEADS,)), dma,
        ],
        compiler_params=pltpu.CompilerParams(
            collective_id=1, has_side_effects=True, vmem_limit_bytes=54272 << 10
        ),
    )(
        text_count, timestep, modulation, norm_gain, latent, stale_kv, text_kv,
        w_qkv.transpose(1, 0, 2), w_out.reshape(HEADS, HD, WIDTH),
    )


def solution(mesh):
    in_specs = (
        P(("batch", "blk"), None),
        P(None, ("batch", "blk"), "section"),
        P(None, "batch", "section"),
        P("batch"),
        P("batch"),
        P(),
        P(None, None, "section"),
        P("section", None),
        P(),
    )
    out_specs = (P(("batch", "blk"), "section"), P(None, ("batch", "blk"), "section"))
    return jax.shard_map(local, mesh=mesh, in_specs=in_specs, out_specs=out_specs, check_vma=False)
```

```python
import functools
import math

import jax
import jax.numpy as jnp
from jax import lax
from jax.experimental import pallas as pl
from jax.experimental.pallas import tpu as pltpu
from jax.sharding import PartitionSpec as P

MESH = pl.DeviceIdType.MESH
HD = 128
NY, NZ = 4, 8
HALF = NZ // 2
HEADS = 3
SECTIONS = 4
TOK = 256
TXT = 512
STEPS = 28
WIDTH = 3072
COLS = WIDTH // SECTIONS
PIECES = 2
ROWS = TOK // PIECES
PARTS = 2
PART = TOK // PARTS
EXTRA = 16
SCORE_SCALE = math.log2(math.e) / math.sqrt(HD)


def kernel(
    text_count, timestep, mod_in, gain_in, latent, stale, text, w_qkv, w_out,
    layer_out, next_cache,
    modulation, gain, lat_v, normed, w_v, text_v, kv, fresh, q_all, acc, top, den,
    o_send, o_recv, att, w_all, branch,
    kv_ss, kv_rs, q_ss, q_rs, w_ss, w_rs, o_ss, o_rs, a_ss, a_rs,
    mod_sem, gain_sem, lat_sem, wq_sem, text_sem, own_sem, cache_sem, wo_sem,
):
    blk = lax.axis_index("blk")
    sec = lax.axis_index("section")
    y, z = blk // NZ, blk % NZ

    def at_y(k):
        return {"blk": ((y + k + NY) % NY) * NZ + z}

    def at_sec(j):
        return {"section": (sec + j) % SECTIONS}

    right = {"blk": y * NZ + (z + 1) % NZ}
    left = {"blk": y * NZ + (z + NZ - 1) % NZ}
    friends = [right, left] + [at_y(k) for k in range(1, NY)] + [at_sec(j) for j in range(1, SECTIONS)]
    barrier = pltpu.get_barrier_semaphore()
    for friend in friends:
        pl.semaphore_signal(barrier, inc=1, device_id=friend, device_id_type=MESH)

    def head_cols(h):
        return pl.ds(h * HD, HD)

    own_copies = [
        pltpu.make_async_copy(stale.at[:, :, head_cols(h)], kv.at[0, h], own_sem.at[h]) for h in range(HEADS)
    ]
    for copy in own_copies:
        copy.start()
    pl.semaphore_wait(barrier, len(friends))
    for copy in own_copies:
        copy.wait()

    def ring(h, d, side, piece):
        if piece < PIECES:
            rows = pl.ds(piece * ROWS, ROWS)
        else:
            rows = pl.ds(side * ROWS + (piece - PIECES) * (ROWS // 2), ROWS // 2)
        into = d if side == 0 else NZ - d
        source = kv.at[0 if d == 1 else d - 1 if side == 0 else NZ - d + 1, h, :, rows, :]
        return pltpu.make_async_remote_copy(
            src_ref=source,
            dst_ref=kv.at[into, h, :, rows, :],
            send_sem=kv_ss.at[side, d, h, piece],
            recv_sem=kv_rs.at[side, d, h, piece],
            device_id=right if side == 0 else left,
            device_id_type=MESH,
        )

    def parts(h, d):
        quarters = h == HEADS - 1 and d >= HALF - 1
        onward = [(s, p) for p in (2, 3) for s in range(2)] if quarters else [(s, s) for s in range(2)]
        return onward + ([(s, 1 - s) for s in range(2)] if d < HALF else [])

    def arrive(h, d):
        onward = parts(h, d + 1) if d < HALF else []
        for side, piece in parts(h, d):
            ring(h, d, side, piece).wait_recv()
            if (side, piece) in onward:
                ring(h, d + 1, side, piece).start()
            elif piece == side and (side, 2) in onward:
                ring(h, d + 1, side, 2).start()
                ring(h, d + 1, side, 3).start()

    for h in range(HEADS):
        for side, piece in parts(h, 1):
            ring(h, 1, side, piece).start()

    def w_send(j):
        to = lax.rem(sec + j, SECTIONS)
        return pltpu.make_async_remote_copy(
            src_ref=w_out.at[:, :, pl.ds(pl.multiple_of(to * COLS, COLS), COLS)],
            dst_ref=w_all.at[:, sec],
            send_sem=w_ss.at[j],
            recv_sem=w_rs.at[j],
            device_id=at_sec(j),
            device_id_type=MESH,
        )

    mod_copy = pltpu.make_async_copy(mod_in, modulation, mod_sem)
    gain_copy = pltpu.make_async_copy(gain_in, gain, gain_sem)
    lat_copy = pltpu.make_async_copy(latent, lat_v, lat_sem)
    for copy in (lat_copy, mod_copy, gain_copy):
        copy.start()
    wq_copies = [pltpu.make_async_copy(w_qkv.at[c], w_v.at[c], wq_sem.at[c]) for c in range(3)]
    for copy in wq_copies:
        copy.start()
    text_copies = [
        pltpu.make_async_copy(text.at[:, :, head_cols(h)], text_v.at[h], text_sem.at[h]) for h in range(HEADS)
    ]
    wo_copy = pltpu.make_async_copy(
        w_out.at[:, :, pl.ds(pl.multiple_of(sec * COLS, COLS), COLS)], w_all.at[:, sec], wo_sem
    )
    for copy in text_copies + [wo_copy]:
        copy.start()

    for j in range(1, SECTIONS):
        w_send(j).start()

    mod_copy.wait()
    def pick_row(rows):
        steps = lax.broadcasted_iota(jnp.int32, rows.shape, 0)
        return jnp.sum(jnp.where(steps == timestep[0], rows.astype(jnp.float32), 0.0), axis=0, keepdims=True)

    shift = pick_row(modulation[:, :WIDTH])
    scale = 1.0 + pick_row(modulation[:, WIDTH : 2 * WIDTH])
    lat_copy.wait()
    gain_copy.wait()

    chunk = 16

    def norm_rows(i, _):
        rows = pl.ds(pl.multiple_of(i * chunk, chunk), chunk)
        x = lat_v[rows, :].astype(jnp.float32)
        centered = x - jnp.mean(x, axis=1, keepdims=True)
        var = jnp.mean(centered * centered, axis=1, keepdims=True)
        normed[rows, :] = (centered * lax.rsqrt(var + 1e-06) * scale + shift).astype(jnp.bfloat16)
        return 0

    lax.fori_loop(0, TOK // chunk, norm_rows, 0)

    def project(c):
        wq_copies[c].wait()
        return jnp.dot(normed[...], w_v[c], preferred_element_type=jnp.float32)

    def head_norm(block, g):
        square = jnp.mean(block * block, axis=-1, keepdims=True)
        return (block * lax.rsqrt(square + 1e-06) * g).astype(jnp.bfloat16)

    def q_send(h, k):
        return pltpu.make_async_remote_copy(
            src_ref=q_all.at[h, 0:TOK, :],
            dst_ref=q_all.at[h, k * TOK : (k + 1) * TOK, :],
            send_sem=q_ss.at[h, k],
            recv_sem=q_rs.at[h, k],
            device_id=at_y(k),
            device_id_type=MESH,
        )

    projected = project(0)
    for h in range(HEADS):
        q_all[h, 0:TOK, :] = head_norm(projected[:, h * HD : (h + 1) * HD], gain[0:1, :])
        for k in range(1, NY):
            q_send(h, k).start()
    arrive(0, 1)
    projected = project(1)
    for h in range(HEADS):
        fresh[h, 0] = head_norm(projected[:, h * HD : (h + 1) * HD], gain[1:2, :])
    arrive(1, 1)
    projected = project(2)
    for h in range(HEADS):
        fresh[h, 1] = projected[:, h * HD : (h + 1) * HD].astype(jnp.bfloat16)
    arrive(2, 1)
    cache_copies = [
        pltpu.make_async_copy(fresh.at[h], next_cache.at[:, :, head_cols(h)], cache_sem.at[h]) for h in range(HEADS)
    ]
    for copy in cache_copies:
        copy.start()

    def attend(h, low, high, blocks, first):
        q = q_all[h, low:high, :]
        logits = []
        for keys, _, live in blocks:
            s = lax.dot_general(keys, q, (((1,), (1,)), ((), ())), preferred_element_type=jnp.float32)
            logits.append(s if live is None else jnp.where(live, s, -jnp.inf))
        best = functools.reduce(jnp.maximum, [jnp.max(s, axis=0, keepdims=True) for s in logits])
        if not first:
            before = top[h, 0:1, low:high]
            best = jnp.maximum(before, best)
        new_acc = new_den = None
        for s, (_, values, _) in zip(logits, blocks):
            p = jnp.exp2((s - best) * SCORE_SCALE)
            part_den = jnp.sum(p, axis=0, keepdims=True)
            part = lax.dot_general(
                values, p.astype(jnp.bfloat16), (((0,), (0,)), ((), ())), preferred_element_type=jnp.float32
            )
            new_acc = part if new_acc is None else new_acc + part
            new_den = part_den if new_den is None else new_den + part_den
        if not first:
            fade = jnp.exp2((before - best) * SCORE_SCALE)
            new_acc = new_acc + acc[h, :, low:high] * fade
            new_den = new_den + den[h, 0:1, low:high] * fade
        acc[h, :, low:high] = new_acc
        den[h, 0:1, low:high] = new_den
        top[h, 0:1, low:high] = best

    def own_step(h):
        for k in range(1, NY):
            q_send(h, k).wait_recv()
        live = lax.broadcasted_iota(jnp.int32, (TXT, TOK), 0) < text_count[0]
        attend(h, 0, TOK, [(fresh[h, 0], fresh[h, 1], None), (text_v[h, 0], text_v[h, 1], live)], True)
        attend(h, TOK, NY * TOK, [(kv[0, h, 0], kv[0, h, 1], None)], True)

    def pair_step(h, d):
        attend(h, 0, NY * TOK, [(kv[i, h, 0], kv[i, h, 1], None) for i in (d, NZ - d)], False)

    def o_copy(h, k, part):
        return pltpu.make_async_remote_copy(
            src_ref=o_send.at[h, k, part],
            dst_ref=o_recv.at[h, k, part],
            send_sem=o_ss.at[h, k, part],
            recv_sem=o_rs.at[h, k, part],
            device_id=at_y(-k),
            device_id_type=MESH,
        )

    def slot_result(h, k, part):
        start = k * TOK + part * PART
        cols = slice(start, start + PART)
        total = den[h, 0:1, cols]
        return acc[h, :, cols] * (1.0 / total), top[h, 0:1, cols] * SCORE_SCALE + jnp.log2(total)

    def rounded(v):
        return v.astype(jnp.bfloat16).astype(jnp.float32)

    def finish(h):
        for part in range(PARTS):
            for k in (2, 1, 3):
                out, lse = slot_result(h, k, part)
                rest = lse - rounded(lse)
                row = lax.broadcasted_iota(jnp.int32, (EXTRA, PART), 0)
                terms = jnp.where(row == 0, lse, jnp.where(row == 1, rest, rest - rounded(rest)))
                o_send[h, k, part, 0:HD, :] = out.astype(jnp.bfloat16)
                o_send[h, k, part, HD:, :] = terms.astype(jnp.bfloat16)
                o_copy(h, k, part).start()

    def last_step(h):
        block = [(kv[HALF, h, 0], kv[HALF, h, 1], None)]
        attend(h, TOK, NY * TOK, block, False)
        finish(h)
        attend(h, 0, TOK, block, False)

    def a_send(h, j, part):
        return pltpu.make_async_remote_copy(
            src_ref=att.at[h, part, sec],
            dst_ref=att.at[h, part, sec],
            send_sem=a_ss.at[h, j, part],
            recv_sem=a_rs.at[h, j, part],
            device_id=at_sec(j),
            device_id_type=MESH,
        )

    def merge(h, part):
        results = [slot_result(h, 0, part)]
        for k in (1, 3, 2):
            o_copy(h, k, part).wait_recv()
            terms = o_recv[h, k, part, HD:, :].astype(jnp.float32)
            lse = terms[0:1, :] + terms[1:2, :] + terms[2:3, :]
            results.append((o_recv[h, k, part, 0:HD, :].astype(jnp.float32), lse))
        best = functools.reduce(jnp.maximum, [lse for _, lse in results])
        weights = [jnp.exp2(lse - best) for _, lse in results]
        inverse = 1.0 / functools.reduce(jnp.add, weights)
        blend = functools.reduce(jnp.add, [o * (w * inverse) for (o, _), w in zip(results, weights)])
        att[h, part, sec] = blend.astype(jnp.bfloat16)
        for j in (2, 1, 3):
            a_send(h, j, part).start()

    def out_project(h, part):
        for j in (1, 3, 2):
            a_send(h, j, part).wait_recv()
        return lax.dot_general(
            att[h, part].reshape(SECTIONS * HD, PART),
            w_all[h].reshape(SECTIONS * HD, COLS),
            (((0,), (0,)), ((), ())),
            preferred_element_type=jnp.float32,
        )

    for copy in text_copies:
        copy.wait()
    own_step(0)
    own_step(1)
    own_step(2)
    arrive(0, 2)
    pair_step(0, 1)
    arrive(1, 2)
    pair_step(1, 1)
    pair_step(2, 1)
    arrive(0, 3)
    pair_step(0, 2)
    pair_step(0, 3)
    arrive(1, 3)
    pair_step(1, 2)
    arrive(0, 4)
    last_step(0)
    arrive(2, 2)
    pair_step(1, 3)
    arrive(1, 4)
    last_step(1)
    pair_step(2, 2)
    arrive(2, 3)
    merge(0, 0)
    merge(0, 1)
    pair_step(2, 3)
    arrive(2, 4)
    last_step(2)
    merge(1, 0)
    merge(1, 1)
    wo_copy.wait()
    for j in range(1, SECTIONS):
        w_send(j).wait_recv()
    columns = pl.ds(pl.multiple_of(sec * COLS, COLS), COLS)
    gate_row = pick_row(modulation[:, pl.ds(pl.multiple_of(2 * WIDTH + sec * COLS, COLS), COLS)])
    for part in range(PARTS):
        branch[part] = out_project(0, part)
    for part in range(PARTS):
        merge(2, part)
    for part in range(PARTS):
        branch[part] += out_project(1, part)
    for part in range(PARTS):
        rows = slice(part * PART, (part + 1) * PART)
        summed = branch[part] + out_project(2, part)
        layer_out[rows, :] = (lat_v[rows, columns].astype(jnp.float32) + gate_row * summed).astype(jnp.bfloat16)

    for h in range(HEADS):
        for d in range(1, HALF + 1):
            for side, piece in parts(h, d):
                ring(h, d, side, piece).wait_send()
        for k in range(1, NY):
            q_send(h, k).wait_send()
            for part in range(PARTS):
                o_copy(h, k, part).wait_send()
        for j in range(1, SECTIONS):
            for part in range(PARTS):
                a_send(h, j, part).wait_send()
    for j in range(1, SECTIONS):
        w_send(j).wait_send()
    for copy in cache_copies:
        copy.wait()


def local(latent, stale_kv, text_kv, text_count, timestep, modulation, w_qkv, w_out, norm_gain):
    vmem = pl.BlockSpec(memory_space=pltpu.VMEM)
    smem = pl.BlockSpec(memory_space=pltpu.SMEM)
    hbm = pl.BlockSpec(memory_space=pltpu.HBM)
    bf16, f32 = jnp.bfloat16, jnp.float32
    dma = pltpu.SemaphoreType.DMA
    return pl.pallas_call(
        kernel,
        out_shape=(
            jax.ShapeDtypeStruct((TOK, COLS), bf16),
            jax.ShapeDtypeStruct((2, TOK, HEADS * HD), bf16),
        ),
        in_specs=[smem, smem, hbm, hbm, hbm, hbm, hbm, hbm, hbm],
        out_specs=(vmem, hbm),
        scratch_shapes=[
            pltpu.VMEM((STEPS, 3 * WIDTH), bf16),
            pltpu.VMEM((2, HD), f32),
            pltpu.VMEM((TOK, WIDTH), bf16),
            pltpu.VMEM((TOK, WIDTH), bf16),
            pltpu.VMEM((3, WIDTH, HEADS * HD), bf16),
            pltpu.VMEM((HEADS, 2, TXT, HD), bf16),
            pltpu.VMEM((NZ, HEADS, 2, TOK, HD), bf16),
            pltpu.VMEM((HEADS, 2, TOK, HD), bf16),
            pltpu.VMEM((HEADS, NY * TOK, HD), bf16),
            pltpu.VMEM((HEADS, HD, NY * TOK), f32),
            pltpu.VMEM((HEADS, 8, NY * TOK), f32),
            pltpu.VMEM((HEADS, 8, NY * TOK), f32),
            pltpu.VMEM((HEADS, NY, PARTS, HD + EXTRA, PART), bf16),
            pltpu.VMEM((HEADS, NY, PARTS, HD + EXTRA, PART), bf16),
            pltpu.VMEM((HEADS, PARTS, SECTIONS, HD, PART), bf16),
            pltpu.VMEM((HEADS, SECTIONS, HD, COLS), bf16),
            pltpu.VMEM((PARTS, PART, COLS), f32),
            dma((2, HALF + 1, HEADS, 4)), dma((2, HALF + 1, HEADS, 4)),
            dma((HEADS, NY)), dma((HEADS, NY)),
            dma((SECTIONS,)), dma((SECTIONS,)),
            dma((HEADS, NY, PARTS)), dma((HEADS, NY, PARTS)),
            dma((HEADS, SECTIONS, PARTS)), dma((HEADS, SECTIONS, PARTS)),
            dma, dma, dma, dma((3,)), dma((HEADS,)), dma((HEADS,)), dma((HEADS,)), dma,
        ],
        compiler_params=pltpu.CompilerParams(
            collective_id=1, has_side_effects=True, vmem_limit_bytes=54272 << 10
        ),
    )(
        text_count, timestep, modulation, norm_gain, latent, stale_kv, text_kv,
        w_qkv.transpose(1, 0, 2), w_out.reshape(HEADS, HD, WIDTH),
    )


def solution(mesh):
    in_specs = (
        P(("batch", "blk"), None),
        P(None, ("batch", "blk"), "section"),
        P(None, "batch", "section"),
        P("batch"),
        P("batch"),
        P(),
        P(None, None, "section"),
        P("section", None),
        P(),
    )
    out_specs = (P(("batch", "blk"), "section"), P(None, ("batch", "blk"), "section"))
    return jax.shard_map(local, mesh=mesh, in_specs=in_specs, out_specs=out_specs, check_vma=False)
```
